32 devices in a mesh: space: 8 (over z, x), vel: 4 (over y, core).
Axes of the slice: x: 2, y: 2, z: 4, core: 2. Of those that a mesh axis runs over, the one named last changes fastest.
Arguments:
- dist: float32 [32, 48, 2304], P('space', 'vel'), may hold values from 0.4 to 18
- inflow: float32 [48, 2304], P('vel'), may hold values from 0.1 to 3
- neighbor: int32 [4, 32], P(None, 'space'), may hold values from 0 to 31, as said below
- face_kind: int32 [4, 32], P(None, 'space'), may hold values from 0 to 2, as said below
- member: int32 [32], P('space'), may hold values 0 or 1
- face_coef: float32 [4, 32], P(None, 'space'), may hold values from 0.02 to 0.12
- face_angles: float32 [2, 4, 32], P(None, None, 'space'), may hold values from -3.140625 to 3.140625
- dir_angles: float32 [2, 6], replicated, may hold values from -3.140625 to 3.140625
- dir_weights: float32 [6], replicated, may hold values from 0.2 to 0.8
- relax_step: float32 [32], P('space'), may hold values from 0.05 to 0.3
- pen_rate: float32 [32], P('space'), may hold values from 0.2 to 1
Outputs:
- new_dist: float32 [32, 48, 2304], P('space', 'vel')
The draws below stay inside these ranges and needn't reach their ends.
Inputs may be any that keep to these rules, and one draw needn't show every extreme that they name: `neighbor`: each face's neighbour is another cell at most 4 cell numbers away, and that distance occurs. `face_kind`: 0 takes the neighbour cell, 1 the inflow state, 2 the cell itself.
All inputs are finite; a program needn't handle non-finite values. No bound on the sum of `member` on one device may be relied on, other than what follows from the above.
Results may differ from the reference program's by a relative error of at most 0.0003.
Values sent between devices are 32-bit elements; how exact they have to be, the bound alone decides.
A program may use at most 128 MiB of HBM per device.

```python
import math
import jax
import jax.numpy as jnp
from jax import lax

NV = 48
NV2 = 2304
NDIR = 6
NFACE = 4
HALO = 4
CELLS = 32


def draw_dist(key, part):
    rough = jax.random.uniform(key, (CELLS, NV, NV2), jnp.float32, -0.7, 0.7)
    points = (2.0 * jnp.arange(NV, dtype=jnp.float32) + 1.0 - NV) / NV
    envelope = jnp.exp(0.55 * (points + 1.0))
    return envelope[None, :, None] * jnp.exp(rough)


def draw_neighbor(key, part):
    first_key, second_key = jax.random.split(key)
    distance = jax.random.randint(first_key, (NFACE, CELLS), 1, HALO + 1)
    heading = 2 * jax.random.randint(second_key, (NFACE, CELLS), 0, 2) - 1
    cells_row = jnp.arange(CELLS, dtype=jnp.int32)[None, :]
    ahead = cells_row + heading * distance
    behind = cells_row - heading * distance
    inside = (ahead >= 0) & (ahead < CELLS)
    chosen = jnp.where(inside, ahead, behind)
    chosen = chosen.at[0, 1].set(0).at[0, CELLS - 2].set(CELLS - 1).at[1, HALO].set(0)
    return chosen.astype(jnp.int32)


def draw_face_kind(key, part):
    rolled = jax.random.randint(key, (NFACE, CELLS), 0, 6)
    kinds = jnp.where(rolled < 4, 0, rolled - 3)
    return kinds.at[0, 0].set(0).at[2, 0].set(1).at[3, 0].set(2).astype(jnp.int32)


def with_ends(result, stream_key, smallest, high):
    dims = result.shape
    index_at = [jax.random.randint(jax.random.fold_in(stream_key, axis), (), 0, dims[axis]) for axis in range(len(dims))]
    result = result.at[tuple(index_at)].set(smallest)
    longest = dims.index(max(dims))
    index_at[longest] = (index_at[longest] + 1) % dims[longest]
    return result.at[tuple(index_at)].set(high)


def steps_of(stream_key, dims, pieces, smallest, top_value):
    factor_of, own = 1.0, jax.random.fold_in(stream_key, 6)
    for position, blocks in pieces:
        steps = jnp.exp(jax.random.uniform(jax.random.fold_in(own, position), (blocks,), jnp.float32, smallest / len(pieces), top_value / len(pieces)))
        factor_of = factor_of * jnp.repeat(steps, dims[position] // blocks).reshape([-1 if axis == position else 1 for axis in range(len(dims))])
    return factor_of


def setup_inputs(seed: int = 0) -> dict:
    splits = jax.random.split(jax.random.key(seed), 12)
    return {
        "dist": draw_dist(jax.random.fold_in(splits[11], 71), 0),
        "inflow": jnp.clip(jnp.exp(math.log(3.0) - 3.4011974 * jax.random.uniform(splits[1], (NV, NV2), jnp.float32) ** steps_of(splits[1], (NV, NV2), ((0, 4),), -0.2, 0.2)), 0.1, 3.0),
        "neighbor": draw_neighbor(jax.random.fold_in(splits[11], 71), 0),
        "face_kind": draw_face_kind(jax.random.fold_in(splits[11], 71), 0),
        "member": with_ends((jax.random.randint(splits[4], (CELLS,), 0, 4) < 3).astype(jnp.int32), jax.random.fold_in(splits[4], 1), 0, 1),
        "face_coef": jnp.clip(0.02 + 0.09999999776482582 * jax.random.uniform(splits[5], (NFACE, CELLS), jnp.float32) ** steps_of(splits[5], (NFACE, CELLS), ((1, 8),), -0.2, 0.2), 0.02, 0.12),
        "face_angles": jnp.clip(jax.random.uniform(splits[6], (2, NFACE, CELLS), jnp.float32, -3.140625, 3.140625), -3.140625, 3.140625),
        "dir_angles": jnp.clip(jax.random.uniform(splits[7], (2, NDIR), jnp.float32, -3.140625, 3.140625), -3.140625, 3.140625),
        "dir_weights": jnp.clip(jnp.exp(jax.random.uniform(splits[8], (NDIR,), jnp.float32, math.log(0.2), math.log(0.8))), 0.2, 0.8),
        "relax_step": jnp.clip(jnp.exp(math.log(0.3) - 1.7917595 * jax.random.uniform(splits[9], (CELLS,), jnp.float32) ** steps_of(splits[9], (CELLS,), ((0, 8),), -0.2, 0.2)), 0.05, 0.3),
        "pen_rate": jnp.clip(jnp.exp(math.log(1.0) - 1.609438 * jax.random.uniform(splits[10], (CELLS,), jnp.float32) ** steps_of(splits[10], (CELLS,), ((0, 8),), -0.2, 0.2)), 0.2, 1.0),
    }


def velocity_grid(points):
    return (2.0 * jnp.arange(points, dtype=jnp.float32) + 1.0 - points) / points


def velocity_parts(first_rows, points, columns):
    column = jnp.arange(columns, dtype=jnp.int32)
    vel_y = ((2.0 * (column // points).astype(jnp.float32) + 1.0 - points) / points)[None, :]
    vel_z = ((2.0 * (column % points).astype(jnp.float32) + 1.0 - points) / points)[None, :]
    return first_rows[:, None], vel_y, vel_z


def frequency(positions, points):
    return ((positions + points // 2) % points) - points // 2


def spectral_kernels(freq_x, freq_y, freq_z, dir_angles, dir_weights, points):
    alive_mask = ((freq_x != -(points // 2)) & (freq_y != -(points // 2)) & (freq_z != -(points // 2))).astype(jnp.float32)
    azimuth = dir_angles[0][:, None, None, None]
    elevation = dir_angles[1][:, None, None, None]
    projection = (jnp.cos(azimuth) * jnp.cos(elevation) * freq_x.astype(jnp.float32)
                  + jnp.sin(azimuth) * jnp.cos(elevation) * freq_y.astype(jnp.float32)
                  + jnp.sin(elevation) * freq_z.astype(jnp.float32))
    shifting = alive_mask * jnp.cos(projection * (2.0 * math.pi / 8.0))
    scaled = projection / points
    smoothing = alive_mask * dir_weights[:, None, None, None] * jnp.exp(-8.0 * scaled * scaled)
    return jnp.concatenate([shifting, smoothing], axis=0)


def moment_sums(values, vel_x, vel_y, vel_z):
    speed_sq = vel_x * vel_x + vel_y * vel_y + vel_z * vel_z
    return (jnp.sum(values, axis=(-2, -1)), jnp.sum(values * vel_x, axis=(-2, -1)),
            jnp.sum(values * vel_y, axis=(-2, -1)), jnp.sum(values * vel_z, axis=(-2, -1)),
            jnp.sum(values * speed_sq, axis=(-2, -1)))


def maxwellian(totals, vel_x, vel_y, vel_z, points):
    particle_amount_local = totals[0][..., None, None]
    mean_flow_first = totals[1][..., None, None] / particle_amount_local
    mean_flow_second = totals[2][..., None, None] / particle_amount_local
    mean_flow_third = totals[3][..., None, None] / particle_amount_local
    motion_work_total = totals[4][..., None, None]
    heat_level = (motion_work_total / particle_amount_local - (mean_flow_first * mean_flow_first + mean_flow_second * mean_flow_second + mean_flow_third * mean_flow_third)) / 3.0
    lattice_spacing = 2.0 / points
    scaling_divisor = particle_amount_local * lattice_spacing ** 3 * (2.0 * math.pi * heat_level) ** (-1.5)
    relative_motion_norm = (vel_x - mean_flow_first) ** 2 + (vel_y - mean_flow_second) ** 2 + (vel_z - mean_flow_third) ** 2
    return scaling_divisor * jnp.exp(-relative_motion_norm / (2.0 * heat_level))


def reference(dist, inflow, neighbor, face_kind, member, face_coef, face_angles, dir_angles, dir_weights, relax_step, pen_rate):
    vel_x, vel_y, vel_z = velocity_parts(velocity_grid(NV), NV, NV2)
    frequencies = frequency(jnp.arange(NV, dtype=jnp.int32), NV)
    kernels = spectral_kernels(frequencies[:, None, None], frequencies[None, :, None], frequencies[None, None, :], dir_angles, dir_weights, NV)

    def one_cell(cell_index):
        own_cell = dist[cell_index]
        nearby = jnp.take(dist, neighbor[:, cell_index], axis=0)
        face_type = face_kind[:, cell_index][:, None, None]
        upwind = jnp.where(face_type == 0, nearby, jnp.where(face_type == 1, inflow[None], own_cell[None]))
        azimuth = face_angles[0, :, cell_index][:, None, None]
        elevation = face_angles[1, :, cell_index][:, None, None]
        normal_dot = (jnp.cos(azimuth) * jnp.cos(elevation) * vel_x[None] + jnp.sin(azimuth) * jnp.cos(elevation) * vel_y[None]
                      + jnp.sin(elevation) * vel_z[None])
        coefficient = face_coef[:, cell_index][:, None, None]
        face_flux = jnp.sum(coefficient * (jnp.maximum(normal_dot, 0.0) * own_cell[None] + jnp.minimum(normal_dot, 0.0) * upwind), axis=0)
        maxwell = maxwellian(moment_sums(own_cell, vel_x, vel_y, vel_z), vel_x, vel_y, vel_z, NV)
        velocity_cube = own_cell.reshape(NV, NV, NV)
        spectrum = jnp.fft.fftn(velocity_cube)
        fields = jnp.real(jnp.fft.ifftn(kernels * spectrum[None], axes=(1, 2, 3)))
        gain_term = jnp.sum(fields[NDIR:] * (fields[:NDIR] - velocity_cube[None]), axis=0).reshape(NV, NV2)
        advanced = own_cell - face_flux + relax_step[cell_index] * (gain_term - pen_rate[cell_index] * (own_cell - maxwell))
        return jnp.where(member[cell_index] == 1, advanced, own_cell)

    return lax.map(one_cell, jnp.arange(CELLS, dtype=jnp.int32))
```

```python
import math

import jax
import jax.numpy as jnp
import numpy as np
from jax import lax
from jax.experimental import pallas as pl
from jax.experimental.pallas import tpu as pltpu
from jax.sharding import PartitionSpec as P

NV = 48
LANES = 128
CHUNK = 8


HIGHEST_PRECISION = lax.Precision.HIGHEST


def extended(shard, sides, width):
    for axis, dim in sides:
        count, length = (lax.axis_size(axis), shard.shape[dim])
        up = [(i, (i + 1) % count) for i in range(count - 1)]
        down = [(j, i) for i, j in up]
        last = lax.slice_in_dim(shard, length - width, length, axis=dim)
        initial = lax.slice_in_dim(shard, 0, width, axis=dim)
        before = lax.ppermute(last, axis, up)
        after = lax.ppermute(initial, axis, down)
        shard = jnp.concatenate([before, shard, after], axis=dim)
    return shard


def velocity_grid(points):
    return (2.0 * jnp.arange(points, dtype=jnp.float32) + 1.0 - points) / points


def velocity_parts(first_rows, points, columns):
    column = jnp.arange(columns, dtype=jnp.int32)
    vel_y = ((2.0 * (column // points).astype(jnp.float32) + 1.0 - points) / points)[None, :]
    vel_z = ((2.0 * (column % points).astype(jnp.float32) + 1.0 - points) / points)[None, :]
    return (first_rows[:, None], vel_y, vel_z)


def moment_sums(values, vel_x, vel_y, vel_z):
    speed_sq = vel_x * vel_x + vel_y * vel_y + vel_z * vel_z
    return (
        jnp.sum(values, axis=(-2, -1)),
        jnp.sum(values * vel_x, axis=(-2, -1)),
        jnp.sum(values * vel_y, axis=(-2, -1)),
        jnp.sum(values * vel_z, axis=(-2, -1)),
        jnp.sum(values * speed_sq, axis=(-2, -1)),
    )


def maxwellian(totals, vel_x, vel_y, vel_z, points):
    particle_amount_local = totals[0][..., None, None]
    mean_flow_first = totals[1][..., None, None] / particle_amount_local
    mean_flow_second = totals[2][..., None, None] / particle_amount_local
    mean_flow_third = totals[3][..., None, None] / particle_amount_local
    motion_work_total = totals[4][..., None, None]
    heat_level = (
        motion_work_total / particle_amount_local
        - (
            mean_flow_first * mean_flow_first
            + mean_flow_second * mean_flow_second
            + mean_flow_third * mean_flow_third
        )
    ) / 3.0
    lattice_spacing = 2.0 / points
    scaling_divisor = (
        particle_amount_local * lattice_spacing**3 * (2.0 * math.pi * heat_level) ** (-1.5)
    )
    relative_motion_norm = (
        (vel_x - mean_flow_first) ** 2
        + (vel_y - mean_flow_second) ** 2
        + (vel_z - mean_flow_third) ** 2
    )
    return scaling_divisor * jnp.exp(-relative_motion_norm / (2.0 * heat_level))


def trig_tables(points):
    half = points // 2
    order = np.arange(points) % half
    is_sine = np.arange(points) >= half
    angle = 2.0 * np.pi * ((order[:, None] * np.arange(points)[None, :]) % points) / points
    cosine, sine = np.cos(angle), np.sin(angle)
    back = np.where(is_sine[:, None], sine, cosine)
    weight = np.where(order == 0, 1.0, 2.0)[:, None] / points
    even = weight * back
    odd = weight * np.where(is_sine[:, None], cosine, -sine)
    dead = (order == 0) & is_sine
    odd[order == 0] = 0.0
    even[dead] = 0.0
    return even, odd, back.T, order


def lane_block(matrix, copies):
    out = np.zeros((LANES, LANES))
    n = matrix.shape[0]
    for row, col in copies:
        out[row * n : (row + 1) * n, col * n : (col + 1) * n] = matrix
    return out


def dot3(a, b):
    return jnp.dot(a, b, precision=lax.Precision.HIGH, preferred_element_type=jnp.float32)


def gain_kernel(
    cube_ref, fz_ref, fyx_ref, iz_ref, iv_ref, freq_ref, lane_ref, dirs_ref, acc_ref,
    y00, y10, y01, y11, h1, h2, h3, h4, ta, tb, tab,
):
    n = NV
    chunks = n // CHUNK

    def forward_yz(i, carry):
        rows = pl.multiple_of(i * (CHUNK * n), CHUNK * n)
        z = dot3(cube_ref[pl.ds(rows, CHUNK * n), :], fz_ref[...])
        for u in range(CHUNK):
            out = dot3(fyx_ref[...], z[u * n : (u + 1) * n, :])
            here = pl.ds(rows + u * n, n)
            y00[here, :] = out[:n, :LANES]
            y10[here, :] = out[n:, :LANES]
            y01[here, :] = out[:n, LANES:]
            y11[here, :] = out[n:, LANES:]
        return carry

    lax.fori_loop(0, chunks, forward_yz, 0)

    def forward_x(i, carry):
        for u in range(CHUNK):
            q = i * CHUNK + u
            pick = pl.ds(q, n, stride=n)
            even = dot3(fyx_ref[:n, :], jnp.concatenate([y00[pick, :], y11[pick, :]], axis=1))
            odd = dot3(fyx_ref[n:, :], jnp.concatenate([y10[pick, :], y01[pick, :]], axis=1))
            g000, g011 = even[:, :LANES], even[:, LANES:]
            g110, g101 = odd[:, :LANES], odd[:, LANES:]
            here = pl.ds(pl.multiple_of(q * n, n), n)
            h1[here, :] = 0.25 * ((g000 - g110) - (g101 + g011))
            h2[here, :] = 0.25 * ((g000 - g110) + (g101 + g011))
            h3[here, :] = 0.25 * ((g000 + g110) - (g101 - g011))
            h4[here, :] = 0.25 * ((g000 + g110) + (g101 - g011))
        return carry

    lax.fori_loop(0, chunks, forward_x, 0)

    turn = 2.0 * math.pi / 8.0
    for pack in range(dirs_ref.shape[0]):
        e_x = dirs_ref[pack, 0:1, :]
        e_y = dirs_ref[pack, 1:2, :]
        e_z = dirs_ref[pack, 2:3, :]
        weight = dirs_ref[pack, 3:4, :]
        a = freq_ref[...] * e_x
        c = lane_ref[...] * e_z
        cos_a, sin_a = jnp.cos(a * turn), jnp.sin(a * turn)
        cos_c, sin_c = jnp.cos(c * turn), jnp.sin(c * turn)
        b_all = freq_ref[...] * e_y
        tab[0] = b_all
        tab[1] = jnp.cos(b_all * turn)
        tab[2] = jnp.sin(b_all * turn)

        def inverse_zx(i, carry):
            packed = []
            for u in range(CHUNK):
                q = i * CHUNK + u
                here = pl.ds(pl.multiple_of(q * n, n), n)
                b = tab[0, pl.ds(q, 1), :]
                cos_b = tab[1, pl.ds(q, 1), :]
                sin_b = tab[2, pl.ds(q, 1), :]
                f1, f2, f3, f4 = h1[here, :], h2[here, :], h3[here, :], h4[here, :]
                cc, ss = cos_a * cos_b, sin_a * sin_b
                sc, cs = sin_a * cos_b, cos_a * sin_b
                shifting = cos_c * ((cc - ss) * (f1 + f2) + (cc + ss) * (f3 + f4)) + sin_c * (
                    (sc + cs) * (f2 - f1) + (sc - cs) * (f4 - f3)
                )
                up, um = a + b, a - b
                smoothing = 0.0
                for kappa, part in ((up + c, f1), (up - c, f2), (um + c, f3), (um - c, f4)):
                    smoothing += jnp.exp(kappa * kappa * (-8.0 / (NV * NV))) * part
                packed.append(jnp.concatenate([shifting, weight * smoothing], axis=1))
            z = dot3(jnp.concatenate(packed, axis=0), iz_ref[...])
            for u in range(CHUNK):
                out = dot3(iv_ref[...], z[u * n : (u + 1) * n, :])
                here = pl.ds(pl.multiple_of((i * CHUNK + u) * n, n), n)
                ta[here, :] = out[:, :LANES]
                tb[here, :] = out[:, LANES:]
            return carry

        lax.fori_loop(0, chunks, inverse_zx, 0)

        def inverse_y(i, carry):
            for u in range(CHUNK):
                q = i * CHUNK + u
                pick = pl.ds(q, n, stride=n)
                out = dot3(iv_ref[...], jnp.concatenate([ta[pick, :], tb[pick, :]], axis=1))
                here = pl.ds(pl.multiple_of(q * n, n), n)
                term = out[:, LANES:] * (out[:, :LANES] - cube_ref[here, :])
                if pack == 0:
                    acc_ref[here, :] = term
                else:
                    acc_ref[here, :] += term
            return carry

        lax.fori_loop(0, chunks, inverse_y, 0)


def collision_gain(cube, dir_angles, dir_weights):
    even, odd, back, order = trig_tables(NV)
    count = dir_angles.shape[1]
    packs = count // 2
    dup = ((0, 0), (0, 1))
    f_z = np.concatenate([lane_block(even.T, dup), lane_block(odd.T, dup)], axis=1)
    diag = lane_block(back.T, ((0, 0), (1, 1)))
    i_z = np.kron(np.eye(2), diag)
    f_yx = np.concatenate([even, odd], axis=0)
    lane = np.zeros((1, LANES))
    lane[0, : 2 * NV] = np.tile(order, 2)
    freq = np.tile(order[:, None], (1, LANES))
    azimuth, elevation = dir_angles[0], dir_angles[1]
    dirs = jnp.stack(
        [
            jnp.cos(azimuth) * jnp.cos(elevation),
            jnp.sin(azimuth) * jnp.cos(elevation),
            jnp.sin(elevation),
            dir_weights,
        ]
    )
    dirs = jnp.repeat(dirs, NV, axis=1).reshape(4, packs, 2 * NV).transpose(1, 0, 2)
    dirs = jnp.pad(dirs, ((0, 0), (0, 0), (0, LANES - 2 * NV)))
    flat = cube.reshape(NV * NV, NV)
    doubled = jnp.concatenate(
        [flat, flat, jnp.zeros((NV * NV, LANES - 2 * NV), jnp.float32)], axis=1
    )
    table = lambda t: jnp.asarray(t, jnp.float32)
    big = pltpu.VMEM((NV * NV, LANES), jnp.float32)
    acc = pl.pallas_call(
        gain_kernel,
        out_shape=jax.ShapeDtypeStruct((NV * NV, LANES), jnp.float32),
        in_specs=[pl.BlockSpec(memory_space=pltpu.VMEM)] * 8,
        out_specs=pl.BlockSpec(memory_space=pltpu.VMEM),
        scratch_shapes=[big] * 10 + [pltpu.VMEM((3, NV, LANES), jnp.float32)],
        compiler_params=pltpu.CompilerParams(vmem_limit_bytes=40 * 1024 * 1024),
        cost_estimate=pl.CostEstimate(
            flops=2 * 10**9, bytes_accessed=4 * 10**6, transcendentals=2 * 10**6
        ),
    )(doubled, table(f_z), table(f_yx), table(i_z), table(back), table(freq), table(lane), dirs)
    return (acc[:, :NV] + acc[:, NV : 2 * NV]).reshape(NV, NV * NV)


def body(
    dist,
    inflow,
    neighbor,
    face_kind,
    member,
    face_coef,
    face_angles,
    dir_angles,
    dir_weights,
    relax_step,
    pen_rate,
):
    cells_dev, slab_rows, columns = dist.shape
    face_count = neighbor.shape[0]
    groups = lax.axis_size("vel")
    vel_index = lax.axis_index("vel")
    grid_points = velocity_grid(NV)
    slab_x = lax.dynamic_slice_in_dim(grid_points, vel_index * slab_rows, slab_rows)
    vel_x, vel_y, vel_z = velocity_parts(slab_x, NV, columns)
    padded = extended(dist, (("space", 0),), cells_dev)
    first_cell = lax.axis_index("space") * cells_dev - cells_dev
    local_slot = neighbor - first_cell
    onehot = (
        local_slot[:, :, None] == jnp.arange(3 * cells_dev, dtype=jnp.int32)[None, None, :]
    ).astype(jnp.float32)
    nearby = jnp.dot(
        onehot.reshape(face_count * cells_dev, 3 * cells_dev),
        padded.reshape(3 * cells_dev, slab_rows * columns),
        precision=HIGHEST_PRECISION,
    ).reshape(face_count, cells_dev, slab_rows, columns)
    face_type = face_kind[:, :, None, None]
    upwind = jnp.where(
        face_type == 0, nearby, jnp.where(face_type == 1, inflow[None, None], dist[None])
    )
    azimuth = face_angles[0][:, :, None, None]
    elevation = face_angles[1][:, :, None, None]
    normal_dot = (
        jnp.cos(azimuth) * jnp.cos(elevation) * vel_x[None, None]
        + jnp.sin(azimuth) * jnp.cos(elevation) * vel_y[None, None]
        + jnp.sin(elevation) * vel_z[None, None]
    )
    coefficient = face_coef[:, :, None, None]
    face_flux = jnp.sum(
        coefficient
        * (jnp.maximum(normal_dot, 0.0) * dist[None] + jnp.minimum(normal_dot, 0.0) * upwind),
        axis=0,
    )
    per_device = cells_dev // groups
    blocks = dist.reshape(groups, per_device, slab_rows, columns)
    whole_cells = lax.all_to_all(blocks, "vel", split_axis=0, concat_axis=2, tiled=True).reshape(
        per_device, NV, columns
    )
    first_slot = vel_index * per_device
    relax_mine = lax.dynamic_slice_in_dim(relax_step, first_slot, per_device)
    pen_mine = lax.dynamic_slice_in_dim(pen_rate, first_slot, per_device)
    full_x, full_y, full_z = velocity_parts(grid_points, NV, columns)

    def one_cell(packed):
        own_cell, relax_one, pen_one = packed
        maxwell = maxwellian(
            moment_sums(own_cell, full_x, full_y, full_z), full_x, full_y, full_z, NV
        )
        gain_term = collision_gain(own_cell.reshape(NV, NV, NV), dir_angles, dir_weights)
        return relax_one * (gain_term - pen_one * (own_cell - maxwell))

    increments = jnp.stack(
        [one_cell((whole_cells[i], relax_mine[i], pen_mine[i])) for i in range(per_device)]
    )
    increment = lax.all_to_all(
        increments.reshape(1, per_device, NV, columns),
        "vel",
        split_axis=2,
        concat_axis=0,
        tiled=True,
    )
    increment = increment.reshape(cells_dev, slab_rows, columns)
    advanced = dist - face_flux + increment
    return jnp.where(member[:, None, None] == 1, advanced, dist)


def solution(mesh):
    placed = (
        P("space", "vel", None),
        P("vel", None),
        P(None, "space"),
        P(None, "space"),
        P("space"),
        P(None, "space"),
        P(None, None, "space"),
        P(),
        P(),
        P("space"),
        P("space"),
    )
    return jax.shard_map(
        body, mesh=mesh, in_specs=placed, out_specs=P("space", "vel", None), check_vma=False
    )
```

```python
import math

import jax
import jax.numpy as jnp
import numpy as np
from jax import lax
from jax.experimental import pallas as pl
from jax.experimental.pallas import tpu as pltpu
from jax.sharding import PartitionSpec as P

NV = 48
LANES = 128
CHUNK = 8


def neighbours(shard, axis):
    count = lax.axis_size(axis)
    up = [(i, i + 1) for i in range(count - 1)]
    down = [(j, i) for i, j in up]
    return lax.ppermute(shard, axis, up), lax.ppermute(shard, axis, down)


def velocity_grid(points):
    return (2.0 * jnp.arange(points, dtype=jnp.float32) + 1.0 - points) / points


def trig_tables(points):
    half = points // 2
    order = np.arange(points) % half
    is_sine = np.arange(points) >= half
    angle = 2.0 * np.pi * ((order[:, None] * np.arange(points)[None, :]) % points) / points
    cosine, sine = np.cos(angle), np.sin(angle)
    back = np.where(is_sine[:, None], sine, cosine)
    weight = np.where(order == 0, 1.0, 2.0)[:, None] / points
    even = weight * back
    odd = weight * np.where(is_sine[:, None], cosine, -sine)
    dead = (order == 0) & is_sine
    odd[order == 0] = 0.0
    even[dead] = 0.0
    return even, odd, back.T, order


def lane_block(matrix, copies):
    out = np.zeros((LANES, LANES))
    n = matrix.shape[0]
    for row, col in copies:
        out[row * n : (row + 1) * n, col * n : (col + 1) * n] = matrix
    return out


def dot3(a, b):
    return jnp.dot(a, b, precision=lax.Precision.HIGH, preferred_element_type=jnp.float32)


def gain_kernel(
    rates_ref, cube_ref, fz_ref, fyx_ref, iz_ref, iv_ref, freq_ref, lane_ref, vel_ref, dirs_ref,
    inc_ref, acc_ref, y00, y10, y01, y11, h1, h2, h3, h4, ta, tb, tab,
):
    n = NV
    chunks = n // CHUNK
    packs = dirs_ref.shape[0]
    vel_y, vel_z, first_copy = vel_ref[0], vel_ref[1], vel_ref[2]

    def moments(q, sums):
        slab = cube_ref[pl.ds(pl.multiple_of(q * n, n), n), :]
        vel_x = (2.0 * q.astype(jnp.float32) + 1.0 - n) / n
        return sums[0] + slab, sums[1] + vel_x * slab, sums[2] + (vel_x * vel_x) * slab

    zero = jnp.zeros((n, LANES), jnp.float32)
    plain, along, squared = lax.fori_loop(0, n, moments, (zero, zero, zero), unroll=4)

    def whole(values):
        return jnp.sum(values * first_copy, keepdims=True)

    density = whole(plain)
    flow_x = whole(along) / density
    flow_y = whole(plain * vel_y) / density
    flow_z = whole(plain * vel_z) / density
    energy = whole(squared + plain * (vel_y * vel_y + vel_z * vel_z))
    heat = (energy / density - (flow_x * flow_x + flow_y * flow_y + flow_z * flow_z)) / 3.0
    wide = 2.0 * math.pi * heat
    peak = density * (2.0 / n) ** 3 / (wide * jnp.sqrt(wide))
    inverse_heat = 1.0 / (2.0 * heat)
    across = (vel_y[:, :n] - flow_y) ** 2 + (vel_z[:, :n] - flow_z) ** 2

    def forward_yz(i, carry):
        rows = pl.multiple_of(i * (CHUNK * n), CHUNK * n)
        z = dot3(cube_ref[pl.ds(rows, CHUNK * n), :], fz_ref[...])
        for u in range(CHUNK):
            out = dot3(fyx_ref[...], z[u * n : (u + 1) * n, :])
            here = pl.ds(rows + u * n, n)
            y00[here, :] = out[:n, :LANES]
            y10[here, :] = out[n:, :LANES]
            y01[here, :] = out[:n, LANES:]
            y11[here, :] = out[n:, LANES:]
        return carry

    lax.fori_loop(0, chunks, forward_yz, 0)

    def forward_x(i, carry):
        for u in range(CHUNK):
            q = i * CHUNK + u
            pick = pl.ds(q, n, stride=n)
            even = dot3(fyx_ref[:n, :], jnp.concatenate([y00[pick, :], y11[pick, :]], axis=1))
            odd = dot3(fyx_ref[n:, :], jnp.concatenate([y10[pick, :], y01[pick, :]], axis=1))
            g000, g011 = even[:, :LANES], even[:, LANES:]
            g110, g101 = odd[:, :LANES], odd[:, LANES:]
            here = pl.ds(pl.multiple_of(q * n, n), n)
            h1[here, :] = 0.25 * ((g000 - g110) - (g101 + g011))
            h2[here, :] = 0.25 * ((g000 - g110) + (g101 + g011))
            h3[here, :] = 0.25 * ((g000 + g110) - (g101 - g011))
            h4[here, :] = 0.25 * ((g000 + g110) + (g101 - g011))
        return carry

    lax.fori_loop(0, chunks, forward_x, 0)

    turn = 2.0 * math.pi / 8.0
    for pack in range(packs):
        azimuth = dirs_ref[pack, 0:1, :]
        elevation = dirs_ref[pack, 1:2, :]
        weight = dirs_ref[pack, 2:3, :]
        e_x = jnp.cos(azimuth) * jnp.cos(elevation)
        e_y = jnp.sin(azimuth) * jnp.cos(elevation)
        e_z = jnp.sin(elevation)
        a = freq_ref[...] * e_x
        c = lane_ref[...] * e_z
        cos_a, sin_a = jnp.cos(a * turn), jnp.sin(a * turn)
        cos_c, sin_c = jnp.cos(c * turn), jnp.sin(c * turn)
        b_all = freq_ref[...] * e_y
        tab[0] = b_all
        tab[1] = jnp.cos(b_all * turn)
        tab[2] = jnp.sin(b_all * turn)

        def inverse_zx(i, carry):
            packed = []
            for u in range(CHUNK):
                q = i * CHUNK + u
                here = pl.ds(pl.multiple_of(q * n, n), n)
                b = tab[0, pl.ds(q, 1), :]
                cos_b = tab[1, pl.ds(q, 1), :]
                sin_b = tab[2, pl.ds(q, 1), :]
                f1, f2, f3, f4 = h1[here, :], h2[here, :], h3[here, :], h4[here, :]
                cc, ss = cos_a * cos_b, sin_a * sin_b
                sc, cs = sin_a * cos_b, cos_a * sin_b
                shifting = cos_c * ((cc - ss) * (f1 + f2) + (cc + ss) * (f3 + f4)) + sin_c * (
                    (sc + cs) * (f2 - f1) + (sc - cs) * (f4 - f3)
                )
                up, um = a + b, a - b
                smoothing = 0.0
                for kappa, part in ((up + c, f1), (up - c, f2), (um + c, f3), (um - c, f4)):
                    smoothing += jnp.exp(kappa * kappa * (-8.0 / (NV * NV))) * part
                packed.append(jnp.concatenate([shifting, weight * smoothing], axis=1))
            z = dot3(jnp.concatenate(packed, axis=0), iz_ref[...])
            for u in range(CHUNK):
                out = dot3(iv_ref[...], z[u * n : (u + 1) * n, :])
                here = pl.ds(pl.multiple_of((i * CHUNK + u) * n, n), n)
                ta[here, :] = out[:, :LANES]
                tb[here, :] = out[:, LANES:]
            return carry

        lax.fori_loop(0, chunks, inverse_zx, 0)

        def inverse_y(i, carry):
            for u in range(CHUNK):
                q = i * CHUNK + u
                pick = pl.ds(q, n, stride=n)
                out = dot3(iv_ref[...], jnp.concatenate([ta[pick, :], tb[pick, :]], axis=1))
                here = pl.ds(pl.multiple_of(q * n, n), n)
                term = out[:, LANES:] * (out[:, :LANES] - cube_ref[here, :])
                if pack == 0:
                    acc_ref[here, :] = term
                elif pack < packs - 1:
                    acc_ref[here, :] += term
                else:
                    total = acc_ref[here, :] + term
                    vel_x = (2.0 * q.astype(jnp.float32) + 1.0 - n) / n
                    apart = (vel_x - flow_x) ** 2 + across
                    maxwell = peak * jnp.exp(-(apart * inverse_heat))
                    drift = cube_ref[here, :n] - maxwell
                    inc_ref[here, :] = rates_ref[0] * (
                        total[:, :n] + total[:, n : 2 * n] - rates_ref[1] * drift
                    )
            return carry

        lax.fori_loop(0, chunks, inverse_y, 0)


def collision_step(cube, rates, dir_angles, dir_weights):
    even, odd, back, order = trig_tables(NV)
    count = dir_angles.shape[1]
    packs = count // 2
    dup = ((0, 0), (0, 1))
    f_z = np.concatenate([lane_block(even.T, dup), lane_block(odd.T, dup)], axis=1)
    diag = lane_block(back.T, ((0, 0), (1, 1)))
    i_z = np.kron(np.eye(2), diag)
    f_yx = np.concatenate([even, odd], axis=0)
    lane = np.zeros((1, LANES))
    lane[0, : 2 * NV] = np.tile(order, 2)
    freq = np.tile(order[:, None], (1, LANES))
    dirs = jnp.concatenate([dir_angles, dir_weights[None]], axis=0)
    dirs = jnp.repeat(dirs, NV, axis=1).reshape(3, packs, 2 * NV).transpose(1, 0, 2)
    dirs = jnp.pad(dirs, ((0, 0), (0, 0), (0, LANES - 2 * NV)))
    speed = (2.0 * np.arange(NV) + 1.0 - NV) / NV
    inside = np.arange(LANES) < NV
    vel = np.zeros((3, NV, LANES))
    vel[0] = speed[:, None]
    vel[1, :, :NV] = speed[None, :]
    vel[2] = inside[None, :]
    flat = cube.reshape(NV * NV, NV)
    doubled = jnp.concatenate(
        [flat, flat, jnp.zeros((NV * NV, LANES - 2 * NV), jnp.float32)], axis=1
    )
    table = lambda t: jnp.asarray(t, jnp.float32)
    big = pltpu.VMEM((NV * NV, LANES), jnp.float32)
    inc = pl.pallas_call(
        gain_kernel,
        out_shape=jax.ShapeDtypeStruct((NV * NV, NV), jnp.float32),
        in_specs=[pl.BlockSpec(memory_space=pltpu.SMEM)]
        + [pl.BlockSpec(memory_space=pltpu.VMEM)] * 9,
        out_specs=pl.BlockSpec(memory_space=pltpu.VMEM),
        scratch_shapes=[big] * 11 + [pltpu.VMEM((3, NV, LANES), jnp.float32)],
        compiler_params=pltpu.CompilerParams(vmem_limit_bytes=40 * 1024 * 1024),
        cost_estimate=pl.CostEstimate(
            flops=2 * 10**9, bytes_accessed=4 * 10**6, transcendentals=2 * 10**6
        ),
    )(
        rates, doubled, table(f_z), table(f_yx), table(i_z), table(back), table(freq),
        table(lane), table(vel), dirs,
    )
    return inc.reshape(NV, NV * NV)


def flux_kernel(
    slot_ref, kind_ref, coef_ref, normal_ref, vel_ref, x_ref, dist_ref, before_ref, after_ref,
    inflow_ref, out_ref,
):
    faces, cells = kind_ref.shape
    vel_y, vel_z, vel_x = vel_ref[0:1, :], vel_ref[1:2, :], x_ref[...]

    def one_cell(c, carry):
        own = dist_ref[c]
        total = jnp.zeros_like(own)
        for k in range(faces):
            slot = slot_ref[k, c]
            kind = kind_ref[k, c]
            low = before_ref[jnp.clip(slot, 0, cells - 1)]
            mid = dist_ref[jnp.clip(slot - cells, 0, cells - 1)]
            high = after_ref[jnp.clip(slot - 2 * cells, 0, cells - 1)]
            nearby = jnp.where(slot < cells, low, jnp.where(slot < 2 * cells, mid, high))
            upwind = jnp.where(kind == 0, nearby, jnp.where(kind == 1, inflow_ref[...], own))
            dot = normal_ref[0, k, c] * vel_x + (
                normal_ref[1, k, c] * vel_y + normal_ref[2, k, c] * vel_z
            )
            total += coef_ref[k, c] * (
                jnp.maximum(dot, 0.0) * own + jnp.minimum(dot, 0.0) * upwind
            )
        out_ref[c] = own - total
        return carry

    lax.fori_loop(0, cells, one_cell, 0)


def transported(dist, before, after, inflow, slot, kind, coef, angles, slab_x):
    cells, rows, columns = dist.shape
    azimuth, elevation = angles[0], angles[1]
    normal = jnp.stack(
        [
            jnp.cos(azimuth) * jnp.cos(elevation),
            jnp.sin(azimuth) * jnp.cos(elevation),
            jnp.sin(elevation),
        ]
    )
    speed = (2.0 * np.arange(NV) + 1.0 - NV) / NV
    vel = np.stack([np.repeat(speed, NV), np.tile(speed, NV)])
    return pl.pallas_call(
        flux_kernel,
        out_shape=jax.ShapeDtypeStruct(dist.shape, jnp.float32),
        in_specs=[pl.BlockSpec(memory_space=pltpu.SMEM)] * 4
        + [pl.BlockSpec(memory_space=pltpu.VMEM)] * 6,
        out_specs=pl.BlockSpec(memory_space=pltpu.VMEM),
        compiler_params=pltpu.CompilerParams(vmem_limit_bytes=24 * 1024 * 1024),
        cost_estimate=pl.CostEstimate(flops=2 * 10**7, bytes_accessed=3 * 10**6, transcendentals=0),
    )(
        slot, kind, coef, normal, jnp.asarray(vel, jnp.float32), slab_x[:, None],
        dist, before, after, inflow,
    )


def body(
    dist,
    inflow,
    neighbor,
    face_kind,
    member,
    face_coef,
    face_angles,
    dir_angles,
    dir_weights,
    relax_step,
    pen_rate,
):
    cells_dev, slab_rows, columns = dist.shape
    groups = lax.axis_size("vel")
    vel_index = lax.axis_index("vel")
    slab_x = lax.dynamic_slice_in_dim(velocity_grid(NV), vel_index * slab_rows, slab_rows)
    per_device = cells_dev // groups
    blocks = dist.reshape(groups, per_device, slab_rows, columns)
    whole_cells = lax.all_to_all(blocks, "vel", split_axis=0, concat_axis=2, tiled=True).reshape(
        per_device, NV, columns
    )
    before, after = neighbours(dist, "space")
    local_slot = neighbor - (lax.axis_index("space") * cells_dev - cells_dev)
    moved = transported(
        dist, before, after, inflow, local_slot, face_kind, face_coef, face_angles, slab_x
    )
    rates = lax.dynamic_slice_in_dim(
        jnp.stack([relax_step, pen_rate], axis=1), vel_index * per_device, per_device
    )
    increments = jnp.stack(
        [
            collision_step(whole_cells[i].reshape(NV, NV, NV), rates[i], dir_angles, dir_weights)
            for i in range(per_device)
        ]
    )
    increment = lax.all_to_all(
        increments.reshape(1, per_device, NV, columns),
        "vel",
        split_axis=2,
        concat_axis=0,
        tiled=True,
    )
    increment = increment.reshape(cells_dev, slab_rows, columns)
    return jnp.where(member[:, None, None] == 1, moved + increment, dist)


def solution(mesh):
    placed = (
        P("space", "vel", None),
        P("vel", None),
        P(None, "space"),
        P(None, "space"),
        P("space"),
        P(None, "space"),
        P(None, None, "space"),
        P(),
        P(),
        P("space"),
        P("space"),
    )
    return jax.shard_map(
        body, mesh=mesh, in_specs=placed, out_specs=P("space", "vel", None), check_vma=False
    )
```

```python
import math

import jax
import jax.numpy as jnp
import numpy as np
from jax import lax
from jax.experimental import pallas as pl
from jax.experimental.pallas import tpu as pltpu
from jax.sharding import PartitionSpec as P

NV = 48
LANES = 128
CHUNK = 8


def neighbours(shard, axis):
    count = lax.axis_size(axis)
    up = [(i, i + 1) for i in range(count - 1)]
    down = [(j, i) for i, j in up]
    return lax.ppermute(shard, axis, up), lax.ppermute(shard, axis, down)


def velocity_grid(points):
    return (2.0 * jnp.arange(points, dtype=jnp.float32) + 1.0 - points) / points


def trig_tables(points):
    half = points // 2
    order = np.arange(points) % half
    is_sine = np.arange(points) >= half
    angle = 2.0 * np.pi * ((order[:, None] * np.arange(points)[None, :]) % points) / points
    cosine, sine = np.cos(angle), np.sin(angle)
    back = np.where(is_sine[:, None], sine, cosine)
    weight = np.where(order == 0, 1.0, 2.0)[:, None] / points
    even = weight * back
    odd = weight * np.where(is_sine[:, None], cosine, -sine)
    dead = (order == 0) & is_sine
    odd[order == 0] = 0.0
    even[dead] = 0.0
    return even, odd, back.T, order


def lane_block(matrix, copies):
    out = np.zeros((LANES, LANES))
    n = matrix.shape[0]
    for row, col in copies:
        out[row * n : (row + 1) * n, col * n : (col + 1) * n] = matrix
    return out


def halves(values):
    high = values.astype(jnp.bfloat16)
    return high, (values - high.astype(jnp.float32)).astype(jnp.bfloat16)


def constant_halves(matrix):
    single = np.asarray(matrix, np.float32)
    high = single.astype(jnp.bfloat16)
    return high, (single - high.astype(np.float32)).astype(jnp.bfloat16)


def right_parts(matrix):
    return jnp.asarray(np.stack(constant_halves(matrix)))


def left_parts(matrix):
    high, low = constant_halves(matrix)
    return jnp.asarray(np.concatenate([high, low, high], axis=1))


def product(a, b):
    return jnp.dot(a, b, preferred_element_type=jnp.float32)


def by_right(values, parts_ref):
    high, low = halves(values)
    main = parts_ref[0]
    return product(high, main) + (product(low, main) + product(high, parts_ref[1]))


def by_left(parts, values):
    high, low = halves(values)
    return product(parts, jnp.concatenate([high, high, low], axis=0))


def gain_kernel(
    rates_ref, cube_ref, fz_ref, fyx_ref, iz_ref, iv_ref, freq_ref, lane_ref, vel_ref, dirs_ref,
    inc_ref, acc_ref, y00, y10, y01, y11, h1, h2, h3, h4, ta, tb, tab,
):
    n = NV
    chunks = n // CHUNK
    packs = dirs_ref.shape[0]
    vel_y, vel_z, first_copy = vel_ref[0], vel_ref[1], vel_ref[2]

    def moments(q, sums):
        slab = cube_ref[pl.ds(pl.multiple_of(q * n, n), n), :]
        vel_x = (2.0 * q.astype(jnp.float32) + 1.0 - n) / n
        return sums[0] + slab, sums[1] + vel_x * slab, sums[2] + (vel_x * vel_x) * slab

    zero = jnp.zeros((n, LANES), jnp.float32)
    plain, along, squared = lax.fori_loop(0, n, moments, (zero, zero, zero), unroll=4)

    def whole(values):
        return jnp.sum(values * first_copy, keepdims=True)

    density = whole(plain)
    flow_x = whole(along) / density
    flow_y = whole(plain * vel_y) / density
    flow_z = whole(plain * vel_z) / density
    energy = whole(squared + plain * (vel_y * vel_y + vel_z * vel_z))
    heat = (energy / density - (flow_x * flow_x + flow_y * flow_y + flow_z * flow_z)) / 3.0
    wide = 2.0 * math.pi * heat
    peak = density * (2.0 / n) ** 3 / (wide * jnp.sqrt(wide))
    inverse_heat = 1.0 / (2.0 * heat)
    across = (vel_y[:, :n] - flow_y) ** 2 + (vel_z[:, :n] - flow_z) ** 2

    def forward_yz(i, carry):
        rows = pl.multiple_of(i * (CHUNK * n), CHUNK * n)
        z = by_right(cube_ref[pl.ds(rows, CHUNK * n), :], fz_ref)
        for u in range(CHUNK):
            out = by_left(fyx_ref[...], z[u * n : (u + 1) * n, :])
            here = pl.ds(rows + u * n, n)
            y00[here, :] = out[:n, :LANES]
            y10[here, :] = out[n:, :LANES]
            y01[here, :] = out[:n, LANES:]
            y11[here, :] = out[n:, LANES:]
        return carry

    lax.fori_loop(0, chunks, forward_yz, 0)

    def forward_x(i, carry):
        for u in range(CHUNK):
            q = i * CHUNK + u
            pick = pl.ds(q, n, stride=n)
            even = by_left(fyx_ref[:n, :], jnp.concatenate([y00[pick, :], y11[pick, :]], axis=1))
            odd = by_left(fyx_ref[n:, :], jnp.concatenate([y10[pick, :], y01[pick, :]], axis=1))
            g000, g011 = even[:, :LANES], even[:, LANES:]
            g110, g101 = odd[:, :LANES], odd[:, LANES:]
            here = pl.ds(pl.multiple_of(q * n, n), n)
            h1[here, :] = 0.25 * ((g000 - g110) - (g101 + g011))
            h2[here, :] = 0.25 * ((g000 - g110) + (g101 + g011))
            h3[here, :] = 0.25 * ((g000 + g110) - (g101 - g011))
            h4[here, :] = 0.25 * ((g000 + g110) + (g101 - g011))
        return carry

    lax.fori_loop(0, chunks, forward_x, 0)

    turn = 2.0 * math.pi / 8.0
    for pack in range(packs):
        azimuth = dirs_ref[pack, 0:1, :]
        elevation = dirs_ref[pack, 1:2, :]
        weight = dirs_ref[pack, 2:3, :]
        e_x = jnp.cos(azimuth) * jnp.cos(elevation)
        e_y = jnp.sin(azimuth) * jnp.cos(elevation)
        e_z = jnp.sin(elevation)
        a = freq_ref[...] * e_x
        c = lane_ref[...] * e_z
        cos_a, sin_a = jnp.cos(a * turn), jnp.sin(a * turn)
        cos_c, sin_c = jnp.cos(c * turn), jnp.sin(c * turn)
        b_all = freq_ref[...] * e_y
        tab[0] = b_all
        tab[1] = jnp.cos(b_all * turn)
        tab[2] = jnp.sin(b_all * turn)

        def inverse_zx(i, carry):
            packed = []
            for u in range(CHUNK):
                q = i * CHUNK + u
                here = pl.ds(pl.multiple_of(q * n, n), n)
                b = tab[0, pl.ds(q, 1), :]
                cos_b = tab[1, pl.ds(q, 1), :]
                sin_b = tab[2, pl.ds(q, 1), :]
                f1, f2, f3, f4 = h1[here, :], h2[here, :], h3[here, :], h4[here, :]
                cc, ss = cos_a * cos_b, sin_a * sin_b
                sc, cs = sin_a * cos_b, cos_a * sin_b
                shifting = cos_c * ((cc - ss) * (f1 + f2) + (cc + ss) * (f3 + f4)) + sin_c * (
                    (sc + cs) * (f2 - f1) + (sc - cs) * (f4 - f3)
                )
                up, um = a + b, a - b
                smoothing = 0.0
                for kappa, part in ((up + c, f1), (up - c, f2), (um + c, f3), (um - c, f4)):
                    smoothing += jnp.exp(kappa * kappa * (-8.0 / (NV * NV))) * part
                packed.append(jnp.concatenate([shifting, weight * smoothing], axis=1))
            z = by_right(jnp.concatenate(packed, axis=0), iz_ref)
            for u in range(CHUNK):
                out = by_left(iv_ref[...], z[u * n : (u + 1) * n, :])
                here = pl.ds(pl.multiple_of((i * CHUNK + u) * n, n), n)
                ta[here, :] = out[:, :LANES]
                tb[here, :] = out[:, LANES:]
            return carry

        lax.fori_loop(0, chunks, inverse_zx, 0)

        def inverse_y(i, carry):
            for u in range(CHUNK):
                q = i * CHUNK + u
                pick = pl.ds(q, n, stride=n)
                out = by_left(iv_ref[...], jnp.concatenate([ta[pick, :], tb[pick, :]], axis=1))
                here = pl.ds(pl.multiple_of(q * n, n), n)
                term = out[:, LANES:] * (out[:, :LANES] - cube_ref[here, :])
                if pack == 0:
                    acc_ref[here, :] = term
                elif pack < packs - 1:
                    acc_ref[here, :] += term
                else:
                    total = acc_ref[here, :] + term
                    vel_x = (2.0 * q.astype(jnp.float32) + 1.0 - n) / n
                    apart = (vel_x - flow_x) ** 2 + across
                    maxwell = peak * jnp.exp(-(apart * inverse_heat))
                    drift = cube_ref[here, :n] - maxwell
                    inc_ref[here, :] = rates_ref[0] * (
                        total[:, :n] + total[:, n : 2 * n] - rates_ref[1] * drift
                    )
            return carry

        lax.fori_loop(0, chunks, inverse_y, 0)


def collision_step(cube, rates, dir_angles, dir_weights):
    even, odd, back, order = trig_tables(NV)
    count = dir_angles.shape[1]
    packs = count // 2
    dup = ((0, 0), (0, 1))
    f_z = np.concatenate([lane_block(even.T, dup), lane_block(odd.T, dup)], axis=1)
    diag = lane_block(back.T, ((0, 0), (1, 1)))
    i_z = np.kron(np.eye(2), diag)
    f_yx = np.concatenate([even, odd], axis=0)
    lane = np.zeros((1, LANES))
    lane[0, : 2 * NV] = np.tile(order, 2)
    freq = np.tile(order[:, None], (1, LANES))
    dirs = jnp.concatenate([dir_angles, dir_weights[None]], axis=0)
    dirs = jnp.repeat(dirs, NV, axis=1).reshape(3, packs, 2 * NV).transpose(1, 0, 2)
    dirs = jnp.pad(dirs, ((0, 0), (0, 0), (0, LANES - 2 * NV)))
    speed = (2.0 * np.arange(NV) + 1.0 - NV) / NV
    inside = np.arange(LANES) < NV
    vel = np.zeros((3, NV, LANES))
    vel[0] = speed[:, None]
    vel[1, :, :NV] = speed[None, :]
    vel[2] = inside[None, :]
    flat = cube.reshape(NV * NV, NV)
    doubled = jnp.concatenate(
        [flat, flat, jnp.zeros((NV * NV, LANES - 2 * NV), jnp.float32)], axis=1
    )
    table = lambda t: jnp.asarray(t, jnp.float32)
    big = pltpu.VMEM((NV * NV, LANES), jnp.float32)
    inc = pl.pallas_call(
        gain_kernel,
        out_shape=jax.ShapeDtypeStruct((NV * NV, NV), jnp.float32),
        in_specs=[pl.BlockSpec(memory_space=pltpu.SMEM)]
        + [pl.BlockSpec(memory_space=pltpu.VMEM)] * 9,
        out_specs=pl.BlockSpec(memory_space=pltpu.VMEM),
        scratch_shapes=[big] * 11 + [pltpu.VMEM((3, NV, LANES), jnp.float32)],
        compiler_params=pltpu.CompilerParams(vmem_limit_bytes=40 * 1024 * 1024),
        cost_estimate=pl.CostEstimate(
            flops=2 * 10**9, bytes_accessed=4 * 10**6, transcendentals=2 * 10**6
        ),
    )(
        rates, doubled, right_parts(f_z), left_parts(f_yx), right_parts(i_z), left_parts(back),
        table(freq),
        table(lane), table(vel), dirs,
    )
    return inc.reshape(NV, NV * NV)


def flux_kernel(
    slot_ref, kind_ref, coef_ref, normal_ref, vel_ref, x_ref, dist_ref, before_ref, after_ref,
    inflow_ref, out_ref,
):
    faces, cells = kind_ref.shape
    vel_y, vel_z, vel_x = vel_ref[0:1, :], vel_ref[1:2, :], x_ref[...]

    def one_cell(c, carry):
        own = dist_ref[c]
        total = jnp.zeros_like(own)
        for k in range(faces):
            slot = slot_ref[k, c]
            kind = kind_ref[k, c]
            low = before_ref[jnp.clip(slot, 0, cells - 1)]
            mid = dist_ref[jnp.clip(slot - cells, 0, cells - 1)]
            high = after_ref[jnp.clip(slot - 2 * cells, 0, cells - 1)]
            nearby = jnp.where(slot < cells, low, jnp.where(slot < 2 * cells, mid, high))
            upwind = jnp.where(kind == 0, nearby, jnp.where(kind == 1, inflow_ref[...], own))
            dot = normal_ref[0, k, c] * vel_x + (
                normal_ref[1, k, c] * vel_y + normal_ref[2, k, c] * vel_z
            )
            total += coef_ref[k, c] * (
                jnp.maximum(dot, 0.0) * own + jnp.minimum(dot, 0.0) * upwind
            )
        out_ref[c] = own - total
        return carry

    lax.fori_loop(0, cells, one_cell, 0)


def transported(dist, before, after, inflow, slot, kind, coef, angles, slab_x):
    cells, rows, columns = dist.shape
    azimuth, elevation = angles[0], angles[1]
    normal = jnp.stack(
        [
            jnp.cos(azimuth) * jnp.cos(elevation),
            jnp.sin(azimuth) * jnp.cos(elevation),
            jnp.sin(elevation),
        ]
    )
    speed = (2.0 * np.arange(NV) + 1.0 - NV) / NV
    vel = np.stack([np.repeat(speed, NV), np.tile(speed, NV)])
    return pl.pallas_call(
        flux_kernel,
        out_shape=jax.ShapeDtypeStruct(dist.shape, jnp.float32),
        in_specs=[pl.BlockSpec(memory_space=pltpu.SMEM)] * 4
        + [pl.BlockSpec(memory_space=pltpu.VMEM)] * 6,
        out_specs=pl.BlockSpec(memory_space=pltpu.VMEM),
        compiler_params=pltpu.CompilerParams(vmem_limit_bytes=24 * 1024 * 1024),
        cost_estimate=pl.CostEstimate(flops=2 * 10**7, bytes_accessed=3 * 10**6, transcendentals=0),
    )(
        slot, kind, coef, normal, jnp.asarray(vel, jnp.float32), slab_x[:, None],
        dist, before, after, inflow,
    )


def body(
    dist,
    inflow,
    neighbor,
    face_kind,
    member,
    face_coef,
    face_angles,
    dir_angles,
    dir_weights,
    relax_step,
    pen_rate,
):
    cells_dev, slab_rows, columns = dist.shape
    groups = lax.axis_size("vel")
    vel_index = lax.axis_index("vel")
    slab_x = lax.dynamic_slice_in_dim(velocity_grid(NV), vel_index * slab_rows, slab_rows)
    per_device = cells_dev // groups
    blocks = dist.reshape(groups, per_device, slab_rows, columns)
    whole_cells = lax.all_to_all(blocks, "vel", split_axis=0, concat_axis=2, tiled=True).reshape(
        per_device, NV, columns
    )
    halo_source, whole_cells = lax.optimization_barrier((dist, whole_cells))
    before, after = neighbours(halo_source, "space")
    local_slot = neighbor - (lax.axis_index("space") * cells_dev - cells_dev)
    moved = transported(
        dist, before, after, inflow, local_slot, face_kind, face_coef, face_angles, slab_x
    )
    rates = lax.dynamic_slice_in_dim(
        jnp.stack([relax_step, pen_rate], axis=1), vel_index * per_device, per_device
    )
    increments = jnp.stack(
        [
            collision_step(whole_cells[i].reshape(NV, NV, NV), rates[i], dir_angles, dir_weights)
            for i in range(per_device)
        ]
    )
    increment = lax.all_to_all(
        increments.reshape(1, per_device, NV, columns),
        "vel",
        split_axis=2,
        concat_axis=0,
        tiled=True,
    )
    increment = increment.reshape(cells_dev, slab_rows, columns)
    return jnp.where(member[:, None, None] == 1, moved + increment, dist)


def solution(mesh):
    placed = (
        P("space", "vel", None),
        P("vel", None),
        P(None, "space"),
        P(None, "space"),
        P("space"),
        P(None, "space"),
        P(None, None, "space"),
        P(),
        P(),
        P("space"),
        P("space"),
    )
    return jax.shard_map(
        body, mesh=mesh, in_specs=placed, out_specs=P("space", "vel", None), check_vma=False
    )
```

```python
import math

import jax
import jax.numpy as jnp
import numpy as np
from jax import lax
from jax.experimental import pallas as pl
from jax.experimental.pallas import tpu as pltpu
from jax.sharding import PartitionSpec as P

NV = 48
LANES = 128
CHUNK = 24


def neighbours(shard, axis):
    count = lax.axis_size(axis)
    up = [(i, i + 1) for i in range(count - 1)]
    down = [(j, i) for i, j in up]
    return lax.ppermute(shard, axis, up), lax.ppermute(shard, axis, down)


def velocity_grid(points):
    return (2.0 * jnp.arange(points, dtype=jnp.float32) + 1.0 - points) / points


def trig_tables(points):
    half = points // 2
    order = np.arange(points) % half
    is_sine = np.arange(points) >= half
    angle = 2.0 * np.pi * ((order[:, None] * np.arange(points)[None, :]) % points) / points
    cosine, sine = np.cos(angle), np.sin(angle)
    back = np.where(is_sine[:, None], sine, cosine)
    weight = np.where(order == 0, 1.0, 2.0)[:, None] / points
    even = weight * back
    odd = weight * np.where(is_sine[:, None], cosine, -sine)
    dead = (order == 0) & is_sine
    odd[order == 0] = 0.0
    even[dead] = 0.0
    return even, odd, back.T, order


def lane_block(matrix, copies):
    out = np.zeros((LANES, LANES))
    n = matrix.shape[0]
    for row, col in copies:
        out[row * n : (row + 1) * n, col * n : (col + 1) * n] = matrix
    return out


def halves(values):
    high = values.astype(jnp.bfloat16)
    return high, (values - high.astype(jnp.float32)).astype(jnp.bfloat16)


def constant_halves(matrix):
    single = np.asarray(matrix, np.float32)
    high = single.astype(jnp.bfloat16)
    return high, (single - high.astype(np.float32)).astype(jnp.bfloat16)


def right_parts(matrix):
    return jnp.asarray(np.stack(constant_halves(matrix)))


def left_parts(matrix):
    high, low = constant_halves(matrix)
    return jnp.asarray(np.concatenate([high, low, high], axis=1))


def product(a, b):
    return jnp.dot(a, b, preferred_element_type=jnp.float32)


def by_right(values, parts_ref):
    high, low = halves(values)
    main = parts_ref[0]
    return product(high, main) + (product(low, main) + product(high, parts_ref[1]))


def by_left(parts, values):
    high, low = halves(values)
    return product(parts, jnp.concatenate([high, high, low], axis=0))


def gain_kernel(
    rates_ref, cube_ref, fz_ref, fyx_ref, iz_ref, iv_ref, freq_ref, lane_ref, vel_ref, dirs_ref,
    inc_ref, acc_ref, y00, y10, y01, y11, h1, h2, h3, h4, ta, tb, tab,
):
    n = NV
    chunks = n // CHUNK
    packs = dirs_ref.shape[0]
    vel_y, vel_z, first_copy = vel_ref[0], vel_ref[1], vel_ref[2]

    def moments(q, sums):
        slab = cube_ref[pl.ds(pl.multiple_of(q * n, n), n), :]
        vel_x = (2.0 * q.astype(jnp.float32) + 1.0 - n) / n
        return sums[0] + slab, sums[1] + vel_x * slab, sums[2] + (vel_x * vel_x) * slab

    zero = jnp.zeros((n, LANES), jnp.float32)
    plain, along, squared = lax.fori_loop(0, n, moments, (zero, zero, zero), unroll=4)

    def whole(values):
        return jnp.sum(values * first_copy, keepdims=True)

    density = whole(plain)
    flow_x = whole(along) / density
    flow_y = whole(plain * vel_y) / density
    flow_z = whole(plain * vel_z) / density
    energy = whole(squared + plain * (vel_y * vel_y + vel_z * vel_z))
    heat = (energy / density - (flow_x * flow_x + flow_y * flow_y + flow_z * flow_z)) / 3.0
    wide = 2.0 * math.pi * heat
    peak = density * (2.0 / n) ** 3 / (wide * jnp.sqrt(wide))
    inverse_heat = 1.0 / (2.0 * heat)
    across = (vel_y[:, :n] - flow_y) ** 2 + (vel_z[:, :n] - flow_z) ** 2

    def forward_yz(i, carry):
        rows = pl.multiple_of(i * (CHUNK * n), CHUNK * n)
        z = by_right(cube_ref[pl.ds(rows, CHUNK * n), :], fz_ref)
        for u in range(CHUNK):
            out = by_left(fyx_ref[...], z[u * n : (u + 1) * n, :])
            here = pl.ds(rows + u * n, n)
            y00[here, :] = out[:n, :LANES]
            y10[here, :] = out[n:, :LANES]
            y01[here, :] = out[:n, LANES:]
            y11[here, :] = out[n:, LANES:]
        return carry

    lax.fori_loop(0, chunks, forward_yz, 0)

    def forward_x(i, carry):
        for u in range(CHUNK):
            q = i * CHUNK + u
            pick = pl.ds(q, n, stride=n)
            even = by_left(fyx_ref[:n, :], jnp.concatenate([y00[pick, :], y11[pick, :]], axis=1))
            odd = by_left(fyx_ref[n:, :], jnp.concatenate([y10[pick, :], y01[pick, :]], axis=1))
            g000, g011 = even[:, :LANES], even[:, LANES:]
            g110, g101 = odd[:, :LANES], odd[:, LANES:]
            here = pl.ds(pl.multiple_of(q * n, n), n)
            h1[here, :] = 0.25 * ((g000 - g110) - (g101 + g011))
            h2[here, :] = 0.25 * ((g000 - g110) + (g101 + g011))
            h3[here, :] = 0.25 * ((g000 + g110) - (g101 - g011))
            h4[here, :] = 0.25 * ((g000 + g110) + (g101 - g011))
        return carry

    lax.fori_loop(0, chunks, forward_x, 0)

    turn = 2.0 * math.pi / 8.0
    for pack in range(packs):
        azimuth = dirs_ref[pack, 0:1, :]
        elevation = dirs_ref[pack, 1:2, :]
        weight = dirs_ref[pack, 2:3, :]
        e_x = jnp.cos(azimuth) * jnp.cos(elevation)
        e_y = jnp.sin(azimuth) * jnp.cos(elevation)
        e_z = jnp.sin(elevation)
        a = freq_ref[...] * e_x
        c = lane_ref[...] * e_z
        cos_a, sin_a = jnp.cos(a * turn), jnp.sin(a * turn)
        cos_c, sin_c = jnp.cos(c * turn), jnp.sin(c * turn)
        b_all = freq_ref[...] * e_y
        tab[0] = b_all
        tab[1] = jnp.cos(b_all * turn)
        tab[2] = jnp.sin(b_all * turn)

        def inverse_zx(i, carry):
            packed = []
            for u in range(CHUNK):
                q = i * CHUNK + u
                here = pl.ds(pl.multiple_of(q * n, n), n)
                b = tab[0, pl.ds(q, 1), :]
                cos_b = tab[1, pl.ds(q, 1), :]
                sin_b = tab[2, pl.ds(q, 1), :]
                f1, f2, f3, f4 = h1[here, :], h2[here, :], h3[here, :], h4[here, :]
                cc, ss = cos_a * cos_b, sin_a * sin_b
                sc, cs = sin_a * cos_b, cos_a * sin_b
                shifting = cos_c * ((cc - ss) * (f1 + f2) + (cc + ss) * (f3 + f4)) + sin_c * (
                    (sc + cs) * (f2 - f1) + (sc - cs) * (f4 - f3)
                )
                up, um = a + b, a - b
                smoothing = 0.0
                for kappa, part in ((up + c, f1), (up - c, f2), (um + c, f3), (um - c, f4)):
                    smoothing += jnp.exp(kappa * kappa * (-8.0 / (NV * NV))) * part
                packed.append(jnp.concatenate([shifting, weight * smoothing], axis=1))
            z = by_right(jnp.concatenate(packed, axis=0), iz_ref)
            for u in range(CHUNK):
                out = by_left(iv_ref[...], z[u * n : (u + 1) * n, :])
                here = pl.ds(pl.multiple_of((i * CHUNK + u) * n, n), n)
                ta[here, :] = out[:, :LANES]
                tb[here, :] = out[:, LANES:]
            return carry

        lax.fori_loop(0, chunks, inverse_zx, 0)

        def inverse_y(i, carry):
            for u in range(CHUNK):
                q = i * CHUNK + u
                pick = pl.ds(q, n, stride=n)
                out = by_left(iv_ref[...], jnp.concatenate([ta[pick, :], tb[pick, :]], axis=1))
                here = pl.ds(pl.multiple_of(q * n, n), n)
                term = out[:, LANES:] * (out[:, :LANES] - cube_ref[here, :])
                if pack == 0:
                    acc_ref[here, :] = term
                elif pack < packs - 1:
                    acc_ref[here, :] += term
                else:
                    total = acc_ref[here, :] + term
                    vel_x = (2.0 * q.astype(jnp.float32) + 1.0 - n) / n
                    apart = (vel_x - flow_x) ** 2 + across
                    maxwell = peak * jnp.exp(-(apart * inverse_heat))
                    drift = cube_ref[here, :n] - maxwell
                    inc_ref[here, :] = rates_ref[0] * (
                        total[:, :n] + total[:, n : 2 * n] - rates_ref[1] * drift
                    )
            return carry

        lax.fori_loop(0, chunks, inverse_y, 0)


def collision_step(cube, rates, dir_angles, dir_weights):
    even, odd, back, order = trig_tables(NV)
    count = dir_angles.shape[1]
    packs = count // 2
    dup = ((0, 0), (0, 1))
    f_z = np.concatenate([lane_block(even.T, dup), lane_block(odd.T, dup)], axis=1)
    diag = lane_block(back.T, ((0, 0), (1, 1)))
    i_z = np.kron(np.eye(2), diag)
    f_yx = np.concatenate([even, odd], axis=0)
    lane = np.zeros((1, LANES))
    lane[0, : 2 * NV] = np.tile(order, 2)
    freq = np.tile(order[:, None], (1, LANES))
    dirs = jnp.concatenate([dir_angles, dir_weights[None]], axis=0)
    dirs = jnp.repeat(dirs, NV, axis=1).reshape(3, packs, 2 * NV).transpose(1, 0, 2)
    dirs = jnp.pad(dirs, ((0, 0), (0, 0), (0, LANES - 2 * NV)))
    speed = (2.0 * np.arange(NV) + 1.0 - NV) / NV
    inside = np.arange(LANES) < NV
    vel = np.zeros((3, NV, LANES))
    vel[0] = speed[:, None]
    vel[1, :, :NV] = speed[None, :]
    vel[2] = inside[None, :]
    flat = cube.reshape(NV * NV, NV)
    doubled = jnp.concatenate(
        [flat, flat, jnp.zeros((NV * NV, LANES - 2 * NV), jnp.float32)], axis=1
    )
    table = lambda t: jnp.asarray(t, jnp.float32)
    big = pltpu.VMEM((NV * NV, LANES), jnp.float32)
    inc = pl.pallas_call(
        gain_kernel,
        out_shape=jax.ShapeDtypeStruct((NV * NV, NV), jnp.float32),
        in_specs=[pl.BlockSpec(memory_space=pltpu.SMEM)]
        + [pl.BlockSpec(memory_space=pltpu.VMEM)] * 9,
        out_specs=pl.BlockSpec(memory_space=pltpu.VMEM),
        scratch_shapes=[big] * 11 + [pltpu.VMEM((3, NV, LANES), jnp.float32)],
        compiler_params=pltpu.CompilerParams(vmem_limit_bytes=40 * 1024 * 1024),
        cost_estimate=pl.CostEstimate(
            flops=2 * 10**9, bytes_accessed=4 * 10**6, transcendentals=2 * 10**6
        ),
    )(
        rates, doubled, right_parts(f_z), left_parts(f_yx), right_parts(i_z), left_parts(back),
        table(freq),
        table(lane), table(vel), dirs,
    )
    return inc.reshape(NV, NV * NV)


def flux_kernel(
    slot_ref, kind_ref, coef_ref, normal_ref, vel_ref, x_ref, dist_ref, before_ref, after_ref,
    inflow_ref, out_ref,
):
    faces, cells = kind_ref.shape
    vel_y, vel_z, vel_x = vel_ref[0:1, :], vel_ref[1:2, :], x_ref[...]

    def one_cell(c, carry):
        own = dist_ref[c]
        total = jnp.zeros_like(own)
        for k in range(faces):
            slot = slot_ref[k, c]
            kind = kind_ref[k, c]
            low = before_ref[jnp.clip(slot, 0, cells - 1)]
            mid = dist_ref[jnp.clip(slot - cells, 0, cells - 1)]
            high = after_ref[jnp.clip(slot - 2 * cells, 0, cells - 1)]
            nearby = jnp.where(slot < cells, low, jnp.where(slot < 2 * cells, mid, high))
            upwind = jnp.where(kind == 0, nearby, jnp.where(kind == 1, inflow_ref[...], own))
            dot = normal_ref[0, k, c] * vel_x + (
                normal_ref[1, k, c] * vel_y + normal_ref[2, k, c] * vel_z
            )
            total += coef_ref[k, c] * (
                jnp.maximum(dot, 0.0) * own + jnp.minimum(dot, 0.0) * upwind
            )
        out_ref[c] = own - total
        return carry

    lax.fori_loop(0, cells, one_cell, 0)


def transported(dist, before, after, inflow, slot, kind, coef, angles, slab_x):
    cells, rows, columns = dist.shape
    azimuth, elevation = angles[0], angles[1]
    normal = jnp.stack(
        [
            jnp.cos(azimuth) * jnp.cos(elevation),
            jnp.sin(azimuth) * jnp.cos(elevation),
            jnp.sin(elevation),
        ]
    )
    speed = (2.0 * np.arange(NV) + 1.0 - NV) / NV
    vel = np.stack([np.repeat(speed, NV), np.tile(speed, NV)])
    return pl.pallas_call(
        flux_kernel,
        out_shape=jax.ShapeDtypeStruct(dist.shape, jnp.float32),
        in_specs=[pl.BlockSpec(memory_space=pltpu.SMEM)] * 4
        + [pl.BlockSpec(memory_space=pltpu.VMEM)] * 6,
        out_specs=pl.BlockSpec(memory_space=pltpu.VMEM),
        compiler_params=pltpu.CompilerParams(vmem_limit_bytes=24 * 1024 * 1024),
        cost_estimate=pl.CostEstimate(flops=2 * 10**7, bytes_accessed=3 * 10**6, transcendentals=0),
    )(
        slot, kind, coef, normal, jnp.asarray(vel, jnp.float32), slab_x[:, None],
        dist, before, after, inflow,
    )


def body(
    dist,
    inflow,
    neighbor,
    face_kind,
    member,
    face_coef,
    face_angles,
    dir_angles,
    dir_weights,
    relax_step,
    pen_rate,
):
    cells_dev, slab_rows, columns = dist.shape
    groups = lax.axis_size("vel")
    vel_index = lax.axis_index("vel")
    slab_x = lax.dynamic_slice_in_dim(velocity_grid(NV), vel_index * slab_rows, slab_rows)
    per_device = cells_dev // groups
    blocks = dist.reshape(groups, per_device, slab_rows, columns)
    whole_cells = lax.all_to_all(blocks, "vel", split_axis=0, concat_axis=2, tiled=True).reshape(
        per_device, NV, columns
    )
    before, after = neighbours(dist, "space")
    local_slot = neighbor - (lax.axis_index("space") * cells_dev - cells_dev)
    moved = transported(
        dist, before, after, inflow, local_slot, face_kind, face_coef, face_angles, slab_x
    )
    rates = lax.dynamic_slice_in_dim(
        jnp.stack([relax_step, pen_rate], axis=1), vel_index * per_device, per_device
    )
    increments = jnp.stack(
        [
            collision_step(whole_cells[i].reshape(NV, NV, NV), rates[i], dir_angles, dir_weights)
            for i in range(per_device)
        ]
    )
    increment = lax.all_to_all(
        increments.reshape(1, per_device, NV, columns),
        "vel",
        split_axis=2,
        concat_axis=0,
        tiled=True,
    )
    increment = increment.reshape(cells_dev, slab_rows, columns)
    return jnp.where(member[:, None, None] == 1, moved + increment, dist)


def solution(mesh):
    placed = (
        P("space", "vel", None),
        P("vel", None),
        P(None, "space"),
        P(None, "space"),
        P("space"),
        P(None, "space"),
        P(None, None, "space"),
        P(),
        P(),
        P("space"),
        P("space"),
    )
    return jax.shard_map(
        body, mesh=mesh, in_specs=placed, out_specs=P("space", "vel", None), check_vma=False
    )
```
